256 devices in a mesh: gz: 4 (over z_lo), angle: 64 (over z_hi, y, x, core).
Axes of the slice: x: 4, y: 4, z: 8 (z_hi: 2, z_lo: 4; z = z_hi * 4 + z_lo), core: 2. Of those that a mesh axis runs over, the one named last changes fastest.
Arguments:
- index: float32 [4, 256, 256], P('gz'), may hold values from 0 to 0.5
- prop_phase: float32 [256, 256], replicated, may hold values from -3.140625 to 3.140625
- entry_field: float32 [4, 256, 2, 256, 256], P('gz', 'angle'), may hold values from -6 to 6
- exit_cotangent: float32 [256, 2, 256, 256], P('angle'), may hold values from -6 to 6
Outputs:
- new_index: float32 [4, 256, 256], P('gz')
The draws below stay inside these ranges and needn't reach their ends.
All inputs are finite; a program needn't handle non-finite values.
Results may differ from the reference program's by a relative error of at most 0.0001.
Values sent between devices are 32-bit elements; how exact they have to be, the bound alone decides.
No kernel may reach another device: no remote copies, remote signals or barrier semaphores. Data moves between devices by JAX's collectives and lax.ppermute only.
A program may use at most 128 MiB of HBM per device.

```python
import jax
import jax.numpy as jnp
from jax import lax

GRID = 256
SL = 1
SLABS = 4
DEPTH = 4
ANGLES = 256


def level_of(own_key, extent, cuts, low, high):
    factor_of = 1.0
    for axis_at, parts in cuts:
        steps = jax.random.uniform(jax.random.fold_in(jax.random.fold_in(own_key, 6), axis_at), (parts,), jnp.float32, low / len(cuts), high / len(cuts))
        factor_of = factor_of * jnp.repeat(jnp.exp(steps), extent[axis_at] // parts).reshape((-1,) + (1,) * (len(extent) - 1 - axis_at))
    return factor_of


def noise(stream_key, extent, width, bound, pieces=(), kind=jnp.bfloat16):
    drawn = jax.random.normal(stream_key, extent, jnp.float32) * width
    if len(pieces) > 0:
        drawn = level_of(stream_key, extent, pieces, -0.22, 0.18) * drawn
    return jnp.clip(drawn, min=-bound, max=bound).astype(kind)


def setup_inputs(seed: int = 0) -> dict:
    keys = jax.random.split(jax.random.key(seed), 5)
    return {
        "index": jnp.clip(0.5 * jax.random.uniform(keys[0], (DEPTH, GRID, GRID), jnp.float32) ** level_of(keys[0], (DEPTH, GRID, GRID), ((0, 4),), -0.2, 0.2), 0.0, 0.5),
        "prop_phase": jnp.clip(jax.random.uniform(keys[1], (GRID, GRID), jnp.float32, -3.140625, 3.140625), -3.140625, 3.140625),
        "entry_field": noise(keys[2], (SLABS, ANGLES, 2, GRID, GRID), 1.0, 6.0, ((0, 4), (1, 64)), jnp.float32),
        "exit_cotangent": noise(keys[3], (ANGLES, 2, GRID, GRID), 1.0, 6.0, ((0, 64),), jnp.float32),
    }


PHASE_GAIN = 2.0
UPDATE_RATE = 4.0


def reference(index, prop_phase, entry_field, exit_cotangent):
    kernel = jnp.exp(1j * prop_phase)
    transmit = jnp.exp(1j * (PHASE_GAIN * index))

    def one_angle(grad_total, angle_no):
        entries = lax.dynamic_index_in_dim(entry_field, angle_no, 1, keepdims=False)
        cotangent = lax.dynamic_index_in_dim(exit_cotangent, angle_no, 0, keepdims=False)
        kept_fields = []
        for slab_no in range(SLABS):
            field_now = entries[slab_no, 0] + 1j * entries[slab_no, 1]
            for layer_no in range(SL):
                depth_no = slab_no * SL + layer_no
                product = transmit[depth_no] * field_now
                kept_fields.append(product)
                field_now = jnp.fft.ifft2(kernel * jnp.fft.fft2(product))
        dual_now = cotangent[0] + 1j * cotangent[1]
        grad_terms = [None] * DEPTH
        for depth_no in range(DEPTH - 1, -1, -1):
            back_field = jnp.fft.ifft2(jnp.conj(kernel) * jnp.fft.fft2(dual_now))
            grad_terms[depth_no] = PHASE_GAIN * jnp.imag(back_field * jnp.conj(kept_fields[depth_no]))
            dual_now = jnp.conj(transmit[depth_no]) * back_field
        return grad_total + jnp.stack(grad_terms), None

    start_total = jnp.zeros((DEPTH, GRID, GRID), jnp.float32)
    grad_total, _ = lax.scan(one_angle, start_total, jnp.arange(ANGLES, dtype=jnp.int32))
    gradient = grad_total / ANGLES
    return jnp.maximum(index - UPDATE_RATE * gradient, 0.0)
```

```python
import jax
import jax.numpy as jnp
import ml_dtypes
import numpy as np
from jax import lax
from jax.experimental import pallas as pl
from jax.experimental.pallas import tpu as pltpu
from jax.sharding import PartitionSpec as P

PHASE_GAIN = 2.0
UPDATE_RATE = 4.0
VMEM_BYTES = 56 * 2**20


def two_terms(matrix):
    matrix = matrix.astype(np.float32)
    high = matrix.astype(ml_dtypes.bfloat16)
    low = (matrix - high.astype(np.float32)).astype(ml_dtypes.bfloat16)
    return high, low, np.zeros_like(low)


def transform_tables(grid_len):
    quarter = grid_len // 4
    j = np.arange(quarter)
    left_fwd, right_fwd, right_inv, left_inv = [], [], [], []

    def as_real(matrix):
        return np.block([[matrix.real, -matrix.imag], [matrix.imag, matrix.real]])

    def on_left(matrix):
        high, low, zero = two_terms(matrix)
        return np.block([[high, high], [low, zero]])

    def on_right(matrix):
        high, low, zero = two_terms(matrix)
        return np.block([[high, low], [high, zero]])

    for residue in range(4):
        turns = (residue * j[None, :]) / grid_len + (j[:, None] * j[None, :] % quarter) / quarter
        fwd = np.exp(-2j * np.pi * turns) / np.sqrt(grid_len)
        inv = np.conj(fwd).T
        flip = np.where(j.repeat(2) < 0, 0.0, 1.0)
        flip[quarter:] = -1.0 if residue in (1, 2) else 1.0
        left_fwd.append(on_left(as_real(fwd)))
        right_fwd.append(on_right(as_real(fwd).T * flip[:, None]))
        right_inv.append(on_right(as_real(inv).T * flip[None, :]))
        left_inv.append(on_left(as_real(inv)))
    return np.stack([np.stack(m) for m in (left_fwd, right_fwd, right_inv, left_inv)])


def split(block):
    high = block.astype(jnp.bfloat16)
    return high, (block - high.astype(jnp.float32)).astype(jnp.bfloat16)


def left_mul(matrix, block):
    both = jnp.dot(
        matrix, jnp.concatenate(split(block), 0), preferred_element_type=jnp.float32
    )
    return both[:128] + both[128:]


def right_mul(block, matrix):
    both = jnp.dot(
        jnp.concatenate(split(block), 1), matrix, preferred_element_type=jnp.float32
    )
    return both[:, :128] + both[:, 128:]


def half_turn(block):
    return pltpu.roll(block, 64, 1)


def adjoint_step(loads, stores, tabs, h_same, h_cross):
    count = len(loads)
    low = lax.broadcasted_iota(jnp.int32, (256 * count, 128), 1) < 64
    sign = jnp.where(low, -1.0, 1.0)

    def rows(a, b):
        return jnp.concatenate([a, b], 0)

    reals, imags = [], []
    for load in loads:
        (x0r, x0i), (x1r, x1i), (x2r, x2i), (x3r, x3i) = [load(p) for p in range(4)]
        s0r, s0i, s1r, s1i = x0r + x2r, x0i + x2i, x1r + x3r, x1i + x3i
        d0r, d0i, d1r, d1i = x0r - x2r, x0i - x2i, x1r - x3r, x1i - x3i
        parts = (
            rows(s0r + s1r, s0i + s1i),
            rows(d0r + d1i, d0i - d1r),
            rows(s0r - s1r, s0i - s1i),
            rows(d0r - d1i, d0i + d1r),
        )
        for p in range(4):
            out = left_mul(tabs[0, p], parts[p])
            reals.append(out[:64])
            imags.append(out[64:])
    yr, yi = jnp.concatenate(reals, 0), jnp.concatenate(imags, 0)

    sr, si = yr[:, :128] + yr[:, 128:], yi[:, :128] + yi[:, 128:]
    dr, di = yr[:, :128] - yr[:, 128:], yi[:, :128] - yi[:, 128:]
    t = jnp.where(low, sr, si)
    u = half_turn(jnp.where(low, si, sr))
    v = half_turn(di)
    a, b = dr + v, dr - v
    parts = (t + u, jnp.where(low, a, b), t - u, jnp.where(low, b, a))
    back = []
    for k in range(4):
        z = right_mul(parts[k], tabs[1, k])
        w = half_turn(z)
        z = jnp.concatenate(
            [
                z[256 * n : 256 * n + 256] * h_same[k] + w[256 * n : 256 * n + 256] * h_cross[k]
                for n in range(count)
            ],
            0,
        )
        back.append(right_mul(z, tabs[2, k]))

    t = back[0] + back[2]
    u = half_turn(back[0] - back[2])
    er, ei = jnp.where(low, t, u), jnp.where(low, u, t)
    fr, fi = back[1] + back[3], half_turn(back[1] - back[3]) * sign
    xr = jnp.concatenate([er + fr, er - fr], 1)
    xi = jnp.concatenate([ei + fi, ei - fi], 1)
    for n in range(count):
        c = []
        for p in range(4):
            at = 256 * n + 64 * p
            out = left_mul(tabs[3, p], rows(xr[at : at + 64], xi[at : at + 64]))
            c.append((out[:64], out[64:]))
        (c0r, c0i), (c1r, c1i), (c2r, c2i), (c3r, c3i) = c
        e0r, e0i, e1r, e1i = c0r + c2r, c0i + c2i, c0r - c2r, c0i - c2i
        f0r, f0i, f1r, f1i = c1r + c3r, c1i + c3i, c3i - c1i, c1r - c3r
        stores[n](0, e0r + f0r, e0i + f0i)
        stores[n](1, e1r + f1r, e1i + f1i)
        stores[n](2, e0r - f0r, e0i - f0i)
        stores[n](3, e1r - f1r, e1i - f1i)


def quarter_at(p):
    return pl.ds(64 * p, 64)


def store_into(ref, angle):
    def store(p, real, imag):
        ref[angle, 0, quarter_at(p), :] = real
        ref[angle, 1, quarter_at(p), :] = imag

    return store


def half_range_cos_sin(turn):
    sq = turn * turn
    c = 1.0 / 479001600.0
    for n in (-1.0 / 3628800.0, 1.0 / 40320.0, -1.0 / 720.0, 1.0 / 24.0, -0.5, 1.0):
        c = c * sq + n
    s = -1.0 / 39916800.0
    for n in (1.0 / 362880.0, -1.0 / 5040.0, 1.0 / 120.0, -1.0 / 6.0, 1.0):
        s = s * sq + n
    return c, s * turn


def first_kernel(dual, phase, tabs, mu, h_same, h_cross, lanes):
    row = lax.broadcasted_iota(jnp.int32, (256, 128), 0)
    lane = lax.broadcasted_iota(jnp.int32, (256, 128), 1)
    col = lane % 64 * 4
    sign = jnp.where(lane < 64, 1.0, -1.0)
    for n in range(2):
        lanes[pl.ds(256 * n, 256), :] = phase[:, pl.ds(128 * n, 128)]
    turn = jnp.concatenate(
        [
            jnp.concatenate([lanes[pl.ds(256 * n + q, 64, stride=4), :] for q in range(4)], 0)
            for n in range(2)
        ],
        1,
    )
    c, s = half_range_cos_sin(0.5 * turn)
    hr, hi = split(1.0 - 2.0 * s * s), split(2.0 * s * c)
    for k in range(4):
        pick = jnp.where(row == col + k, 1.0, 0.0).astype(jnp.bfloat16)
        same, cross = [
            sum(jnp.dot(term, pick, preferred_element_type=jnp.float32) for term in h)
            for h in (hr, hi)
        ]
        h_same[k] = same
        h_cross[k] = cross * sign

    def load_from(angle):
        return lambda p: (dual[angle, 0, quarter_at(p), :], dual[angle, 1, quarter_at(p), :])

    count = dual.shape[0]
    adjoint_step(
        [load_from(n) for n in range(count)],
        [store_into(mu, n) for n in range(count)],
        tabs,
        h_same,
        h_cross,
    )


def rest_kernel(mu_in, h_same, h_cross, tabs, entry, own, near, mid, far, keep, send, mu, tr, ti):
    count = mu_in.shape[0]
    mu[...] = mu_in[...]
    left = 3 - lax.axis_index("gz")

    def set_t(ref):
        c, s = half_range_cos_sin(PHASE_GAIN * ref[...])
        tr[...] = c
        ti[...] = s

    def load_from(angle):
        def load(p):
            at = quarter_at(p)
            r, i = mu[angle, 0, at, :], mu[angle, 1, at, :]
            return tr[at, :] * r + ti[at, :] * i, tr[at, :] * i - ti[at, :] * r

        return load

    def one_slab(step, carry):
        ahead = left - step
        for distance, ref in ((3, far), (2, mid), (1, near)):
            pl.when(ahead == distance)(lambda ref=ref: set_t(ref))
        adjoint_step(
            [load_from(n) for n in range(count)],
            [store_into(mu, n) for n in range(count)],
            tabs,
            h_same,
            h_cross,
        )
        return carry

    lax.fori_loop(0, left, one_slab, 0)
    set_t(own)
    other = 1 - lax.axis_index("angle") % 2

    def terms(at):
        gr = gi = 0.0
        for n in range(count):
            r, i = mu[n, 0, at, :], mu[n, 1, at, :]
            er, ei = entry[n, 0, at, :], entry[n, 1, at, :]
            gr += r * er + i * ei
            gi += i * er - r * ei
        return PHASE_GAIN * (tr[at, :] * gi - ti[at, :] * gr)

    for at in range(0, 128, 32):
        keep[pl.ds(at, 32), :] = terms(pl.ds(pl.multiple_of(128 - 128 * other + at, 32), 32))
        send[pl.ds(at, 32), :] = terms(pl.ds(pl.multiple_of(128 * other + at, 32), 32))


def call(kernel, out_shape, scratch=()):
    return pl.pallas_call(
        kernel,
        out_shape=out_shape,
        scratch_shapes=list(scratch),
        compiler_params=pltpu.CompilerParams(vmem_limit_bytes=VMEM_BYTES),
    )


def f32(*shape):
    return jax.ShapeDtypeStruct(shape, jnp.float32)


def angle_pairs(partner):
    pairs = []
    for n in range(64):
        z, y, x, c = partner(n // 32, n // 8 % 4, n // 2 % 4, n % 2)
        pairs.append((n, z * 32 + y * 8 + x * 2 + c))
    return pairs


def per_device(index, prop_phase, entry_field, exit_cotangent):
    count = exit_cotangent.shape[0]
    tabs = jnp.asarray(transform_tables(256))
    own = index[0]
    near, mid, far = [
        lax.ppermute(own, "gz", [(n, n - by) for n in range(by, 4)]) for by in (1, 2, 3)
    ]
    mu, h_same, h_cross = call(
        first_kernel,
        (f32(count, 2, 256, 256), f32(4, 256, 128), f32(4, 256, 128)),
        (pltpu.VMEM((512, 128), jnp.float32),),
    )(exit_cotangent, prop_phase, tabs)
    plane = pltpu.VMEM((256, 256), jnp.float32)
    keep, send = call(
        rest_kernel,
        (f32(128, 256), f32(128, 256)),
        (pltpu.VMEM((count, 2, 256, 256), jnp.float32), plane, plane),
    )(mu, h_same, h_cross, tabs, entry_field[0], own, near, mid, far)

    core = lax.axis_index("angle") % 2
    swap = angle_pairs(lambda z, y, x, c: (z, y, x, 1 - c))
    total = keep + lax.ppermute(send, "angle", swap)
    for partner in (
        lambda z, y, x, c: (z, y, x ^ 1, c),
        lambda z, y, x, c: (z, y, 3 - x, c),
        lambda z, y, x, c: (z, y ^ 1, x, c),
        lambda z, y, x, c: (z, 3 - y, x, c),
        lambda z, y, x, c: (1 - z, y, x, c),
    ):
        total = total + lax.ppermute(total, "angle", angle_pairs(partner))
    angles = count * lax.axis_size("angle")
    mine = lax.dynamic_slice_in_dim(own, core * 128, 128, 0)
    new = jnp.maximum(mine - UPDATE_RATE * (total / angles), 0.0)
    other = lax.ppermute(new, "angle", swap)
    return jnp.where(
        core == 0, jnp.concatenate([new, other], 0), jnp.concatenate([other, new], 0)
    )[None]


def solution(mesh):
    return jax.shard_map(
        per_device,
        mesh=mesh,
        in_specs=(
            P("gz", None, None),
            P(),
            P("gz", "angle", None, None, None),
            P("angle", None, None, None),
        ),
        out_specs=P("gz", None, None),
        check_vma=False,
    )
```

```python
import jax
import jax.numpy as jnp
import ml_dtypes
import numpy as np
from jax import lax
from jax.experimental import pallas as pl
from jax.experimental.pallas import tpu as pltpu
from jax.sharding import PartitionSpec as P

PHASE_GAIN = 2.0
UPDATE_RATE = 4.0
VMEM_BYTES = 28 * 2**20


def two_terms(matrix):
    matrix = matrix.astype(np.float32)
    high = matrix.astype(ml_dtypes.bfloat16)
    low = (matrix - high.astype(np.float32)).astype(ml_dtypes.bfloat16)
    return high, low, np.zeros_like(low)


def transform_tables(grid_len):
    quarter = grid_len // 4
    j = np.arange(quarter)
    left_fwd, right_fwd, right_inv, left_inv = [], [], [], []

    def as_real(matrix):
        return np.block([[matrix.real, -matrix.imag], [matrix.imag, matrix.real]])

    def on_left(matrix):
        high, low, zero = two_terms(matrix)
        return np.block([[high, high], [low, zero]])

    def on_right(matrix):
        high, low, zero = two_terms(matrix)
        return np.block([[high, low], [high, zero]])

    for residue in range(4):
        turns = (residue * j[None, :]) / grid_len + (j[:, None] * j[None, :] % quarter) / quarter
        fwd = np.exp(-2j * np.pi * turns) / np.sqrt(grid_len)
        inv = np.conj(fwd).T
        flip = np.where(j.repeat(2) < 0, 0.0, 1.0)
        flip[quarter:] = -1.0 if residue in (1, 2) else 1.0
        left_fwd.append(on_left(as_real(fwd)))
        right_fwd.append(on_right(as_real(fwd).T * flip[:, None]))
        right_inv.append(on_right(as_real(inv).T * flip[None, :]))
        left_inv.append(on_left(as_real(inv)))
    return np.stack([np.stack(m) for m in (left_fwd, right_fwd, right_inv, left_inv)])


def split(block):
    high = block.astype(jnp.bfloat16)
    return high, (block - high.astype(jnp.float32)).astype(jnp.bfloat16)


def left_mul(matrix, block):
    both = jnp.dot(
        matrix, jnp.concatenate(split(block), 0), preferred_element_type=jnp.float32
    )
    return both[:128] + both[128:]


def right_mul(block, matrix):
    both = jnp.dot(
        jnp.concatenate(split(block), 1), matrix, preferred_element_type=jnp.float32
    )
    return both[:, :128] + both[:, 128:]


def half_turn(block):
    return pltpu.roll(block, 64, 1)


def adjoint_step(loads, stores, tabs, h_same, h_cross):
    count = len(loads)
    low = lax.broadcasted_iota(jnp.int32, (256 * count, 128), 1) < 64
    sign = jnp.where(low, -1.0, 1.0)

    def rows(a, b):
        return jnp.concatenate([a, b], 0)

    reals, imags = [], []
    for load in loads:
        (x0r, x0i), (x1r, x1i), (x2r, x2i), (x3r, x3i) = [load(p) for p in range(4)]
        s0r, s0i, s1r, s1i = x0r + x2r, x0i + x2i, x1r + x3r, x1i + x3i
        d0r, d0i, d1r, d1i = x0r - x2r, x0i - x2i, x1r - x3r, x1i - x3i
        parts = (
            rows(s0r + s1r, s0i + s1i),
            rows(d0r + d1i, d0i - d1r),
            rows(s0r - s1r, s0i - s1i),
            rows(d0r - d1i, d0i + d1r),
        )
        for p in range(4):
            out = left_mul(tabs[0, p], parts[p])
            reals.append(out[:64])
            imags.append(out[64:])
    yr, yi = jnp.concatenate(reals, 0), jnp.concatenate(imags, 0)

    sr, si = yr[:, :128] + yr[:, 128:], yi[:, :128] + yi[:, 128:]
    dr, di = yr[:, :128] - yr[:, 128:], yi[:, :128] - yi[:, 128:]
    t = jnp.where(low, sr, si)
    u = half_turn(jnp.where(low, si, sr))
    v = half_turn(di)
    a, b = dr + v, dr - v
    parts = (t + u, jnp.where(low, a, b), t - u, jnp.where(low, b, a))
    back = []
    for k in range(4):
        z = right_mul(parts[k], tabs[1, k])
        w = half_turn(z)
        z = jnp.concatenate(
            [
                z[256 * n : 256 * n + 256] * h_same[k] + w[256 * n : 256 * n + 256] * h_cross[k]
                for n in range(count)
            ],
            0,
        )
        back.append(right_mul(z, tabs[2, k]))

    t = back[0] + back[2]
    u = half_turn(back[0] - back[2])
    er, ei = jnp.where(low, t, u), jnp.where(low, u, t)
    fr, fi = back[1] + back[3], half_turn(back[1] - back[3]) * sign
    xr = jnp.concatenate([er + fr, er - fr], 1)
    xi = jnp.concatenate([ei + fi, ei - fi], 1)
    for n in range(count):
        c = []
        for p in range(4):
            at = 256 * n + 64 * p
            out = left_mul(tabs[3, p], rows(xr[at : at + 64], xi[at : at + 64]))
            c.append((out[:64], out[64:]))
        (c0r, c0i), (c1r, c1i), (c2r, c2i), (c3r, c3i) = c
        e0r, e0i, e1r, e1i = c0r + c2r, c0i + c2i, c0r - c2r, c0i - c2i
        f0r, f0i, f1r, f1i = c1r + c3r, c1i + c3i, c3i - c1i, c1r - c3r
        stores[n](0, e0r + f0r, e0i + f0i)
        stores[n](1, e1r + f1r, e1i + f1i)
        stores[n](2, e0r - f0r, e0i - f0i)
        stores[n](3, e1r - f1r, e1i - f1i)


def quarter_at(p):
    return pl.ds(64 * p, 64)


def store_into(ref, angle):
    def store(p, real, imag):
        ref[angle, 0, quarter_at(p), :] = real
        ref[angle, 1, quarter_at(p), :] = imag

    return store


def half_range_cos_sin(turn):
    sq = turn * turn
    c = 1.0 / 479001600.0
    for n in (-1.0 / 3628800.0, 1.0 / 40320.0, -1.0 / 720.0, 1.0 / 24.0, -0.5, 1.0):
        c = c * sq + n
    s = -1.0 / 39916800.0
    for n in (1.0 / 362880.0, -1.0 / 5040.0, 1.0 / 120.0, -1.0 / 6.0, 1.0):
        s = s * sq + n
    return c, s * turn


def start_all(pairs, sems):
    copies = [pltpu.make_async_copy(a, b, sems.at[n]) for n, (a, b) in enumerate(pairs)]
    for copy in copies:
        copy.start()
    return copies


def first_kernel(dual, phase, tabs, mu, h_same, h_cross, lanes):
    row = lax.broadcasted_iota(jnp.int32, (256, 128), 0)
    lane = lax.broadcasted_iota(jnp.int32, (256, 128), 1)
    col = lane % 64 * 4
    sign = jnp.where(lane < 64, 1.0, -1.0)
    for n in range(2):
        lanes[pl.ds(256 * n, 256), :] = phase[:, pl.ds(128 * n, 128)]
    turn = jnp.concatenate(
        [
            jnp.concatenate([lanes[pl.ds(256 * n + q, 64, stride=4), :] for q in range(4)], 0)
            for n in range(2)
        ],
        1,
    )
    c, s = half_range_cos_sin(0.5 * turn)
    hr, hi = split(1.0 - 2.0 * s * s), split(2.0 * s * c)
    for k in range(4):
        pick = jnp.where(row == col + k, 1.0, 0.0).astype(jnp.bfloat16)
        same, cross = [
            sum(jnp.dot(term, pick, preferred_element_type=jnp.float32) for term in h)
            for h in (hr, hi)
        ]
        h_same[k] = same
        h_cross[k] = cross * sign

    def load_from(angle):
        return lambda p: (dual[angle, 0, quarter_at(p), :], dual[angle, 1, quarter_at(p), :])

    count = dual.shape[0]
    adjoint_step(
        [load_from(n) for n in range(count)],
        [store_into(mu, n) for n in range(count)],
        tabs,
        h_same,
        h_cross,
    )


def rest_kernel(
    mu_in, entry_in, h_same, h_cross, tabs, own, got, swapped, near, near_swapped,
    keep, send, mu, entry, tr, ti, sems,
):
    count = mu.shape[0]
    mu_copy, entry_copy = start_all(((mu_in, mu), (entry_in, entry)), sems)
    left = 3 - lax.axis_index("gz")
    core = lax.axis_index("angle") % 2

    def set_t(ref, at=slice(None)):
        c, s = half_range_cos_sin(PHASE_GAIN * ref[...])
        tr[at, :] = c
        ti[at, :] = s

    def set_t_for(step):
        one_above = (left != 2) & (left - step == 1)
        here = (step % 2) == core
        pl.when(~one_above & here)(lambda: set_t(got))
        pl.when(~one_above & ~here)(lambda: set_t(swapped))

        @pl.when(one_above)
        def _():
            set_t(near, pl.ds(pl.multiple_of(core * 128, 128), 128))
            set_t(near_swapped, pl.ds(pl.multiple_of(128 - core * 128, 128), 128))

    def load_from(angle):
        def load(p):
            at = quarter_at(p)
            r, i = mu[angle, 0, at, :], mu[angle, 1, at, :]
            return tr[at, :] * r + ti[at, :] * i, tr[at, :] * i - ti[at, :] * r

        return load

    set_t_for(0)
    mu_copy.wait()

    def one_slab(step, carry):
        pl.when(step > 0)(lambda: set_t_for(step))
        adjoint_step(
            [load_from(n) for n in range(count)],
            [store_into(mu, n) for n in range(count)],
            tabs,
            h_same,
            h_cross,
        )
        return carry

    lax.fori_loop(0, left, one_slab, 0)
    set_t(own)
    entry_copy.wait()

    def terms(at):
        gr = gi = 0.0
        for n in range(count):
            r, i = mu[n, 0, at, :], mu[n, 1, at, :]
            er, ei = entry[n, 0, at, :], entry[n, 1, at, :]
            gr += r * er + i * ei
            gi += i * er - r * ei
        return PHASE_GAIN * (tr[at, :] * gi - ti[at, :] * gr)

    for at in range(0, 128, 32):
        keep[pl.ds(at, 32), :] = terms(pl.ds(pl.multiple_of(core * 128 + at, 32), 32))
        send[pl.ds(at, 32), :] = terms(pl.ds(pl.multiple_of(128 - core * 128 + at, 32), 32))


def call(kernel, in_hbm, out_shape, scratch):
    return pl.pallas_call(
        kernel,
        out_shape=out_shape,
        in_specs=[pl.BlockSpec(memory_space=pl.ANY if far else pltpu.VMEM) for far in in_hbm],
        scratch_shapes=list(scratch),
        compiler_params=pltpu.CompilerParams(vmem_limit_bytes=VMEM_BYTES),
    )


def f32(*shape):
    return jax.ShapeDtypeStruct(shape, jnp.float32)


def angle_pairs(partner):
    pairs = []
    for n in range(64):
        z, y, x, c = partner(n // 32, n // 8 % 4, n // 2 % 4, n % 2)
        pairs.append((n, z * 32 + y * 8 + x * 2 + c))
    return pairs


def slab_pairs(moves):
    pairs = []
    for gz, core, gz_to, core_to, flip in moves:
        for n in range(core, 64, 2):
            pairs.append((gz * 64 + n, gz_to * 64 + ((n - core + core_to) ^ (32 * flip))))
    return pairs


def per_device(index, prop_phase, entry_field, exit_cotangent):
    count = exit_cotangent.shape[0]
    tabs = jnp.asarray(transform_tables(256))
    own = index[0]
    core = lax.axis_index("angle") % 2
    swap = angle_pairs(lambda z, y, x, c: (z, y, x, 1 - c))
    got = lax.ppermute(
        own,
        ("gz", "angle"),
        slab_pairs(((3, 0, 0, 0, 1), (2, 0, 0, 1, 0), (3, 1, 1, 0, 1), (2, 1, 1, 1, 0))),
    )
    mine = lax.dynamic_slice_in_dim(own, core * 128, 128, 0)
    near = lax.ppermute(
        mine,
        ("gz", "angle"),
        slab_pairs(((1, 0, 0, 0, 0), (1, 1, 0, 1, 0), (3, 0, 2, 0, 0), (3, 1, 2, 1, 0))),
    )
    field = (count, 2, 256, 256)
    h_shape = (4, 256, 128)
    mu, h_same, h_cross = call(
        first_kernel,
        (False,) * 3,
        (f32(*field), f32(*h_shape), f32(*h_shape)),
        [pltpu.VMEM((512, 128), jnp.float32)],
    )(exit_cotangent, prop_phase, tabs)
    got, near, mu = lax.optimization_barrier((got, near, mu))
    swapped = lax.ppermute(got, "angle", swap)
    near_swapped = lax.ppermute(near, "angle", swap)
    fields = pltpu.VMEM(field, jnp.float32)
    plane = pltpu.VMEM((256, 256), jnp.float32)
    keep, send = call(
        rest_kernel,
        (True,) * 2 + (False,) * 8,
        (f32(128, 256), f32(128, 256)),
        [fields, fields, plane, plane, pltpu.SemaphoreType.DMA((2,))],
    )(mu, entry_field[0], h_same, h_cross, tabs, own, got, swapped, near, near_swapped)

    total = keep + lax.ppermute(send, "angle", swap)
    for partner in (
        lambda z, y, x, c: (z, y, x ^ 1, c),
        lambda z, y, x, c: (z, y, 3 - x, c),
        lambda z, y, x, c: (z, y ^ 1, x, c),
        lambda z, y, x, c: (z, 3 - y, x, c),
        lambda z, y, x, c: (1 - z, y, x, c),
    ):
        total = total + lax.ppermute(total, "angle", angle_pairs(partner))
    angles = count * lax.axis_size("angle")
    new = jnp.maximum(mine - UPDATE_RATE * (total / angles), 0.0)
    other = lax.ppermute(new, "angle", swap)
    return jnp.where(
        core == 0, jnp.concatenate([new, other], 0), jnp.concatenate([other, new], 0)
    )[None]


def solution(mesh):
    return jax.shard_map(
        per_device,
        mesh=mesh,
        in_specs=(
            P("gz", None, None),
            P(),
            P("gz", "angle", None, None, None),
            P("angle", None, None, None),
        ),
        out_specs=P("gz", None, None),
        check_vma=False,
    )
```

```python
import math

import jax
import jax.numpy as jnp
from jax import lax
from jax.experimental import pallas as pl
from jax.experimental.pallas import tpu as pltpu
from jax.sharding import PartitionSpec as P

PHASE_GAIN = 2.0
UPDATE_RATE = 4.0
VMEM_BYTES = 28 * 2**20


def tables_kernel(tabs):
    row = lax.broadcasted_iota(jnp.int32, (128, 128), 0)
    lane = lax.broadcasted_iota(jnp.int32, (128, 128), 1)
    zero = jnp.zeros((128, 128), jnp.bfloat16)
    for n in range(4):
        for which in range(2):
            m, j = (row % 64, lane % 64) if which == 0 else (lane % 64, row % 64)
            turn = (n * j + 4 * m * j + 128) % 256 - 128
            c, s = half_range_cos_sin(turn.astype(jnp.float32) * (math.pi / 256.0))
            cos, sin = (1.0 - 2.0 * s * s) / 16.0, 2.0 * s * c / 16.0
            upper, right = row < 64, lane >= 64
            cross = jnp.where(upper, sin, -sin)
            real = jnp.where(upper != right, cos, cross if which == 0 else -cross)
            for to in ((0, 2), (3, 1))[which]:
                flipped = real
                if n in (1, 2) and to in (1, 2):
                    flipped = jnp.where((row if to == 1 else lane) < 64, real, -real)
                high, low = split(flipped)
                on_left = to in (0, 3)
                tabs[to, n, :128, :128] = high
                tabs[to, n, :128, 128:] = high if on_left else low
                tabs[to, n, 128:, :128] = low if on_left else high
                tabs[to, n, 128:, 128:] = zero


def split(block):
    high = block.astype(jnp.bfloat16)
    return high, (block - high.astype(jnp.float32)).astype(jnp.bfloat16)


def left_mul(matrix, block):
    both = jnp.dot(
        matrix, jnp.concatenate(split(block), 0), preferred_element_type=jnp.float32
    )
    return both[:128] + both[128:]


def right_mul(block, matrix):
    both = jnp.dot(
        jnp.concatenate(split(block), 1), matrix, preferred_element_type=jnp.float32
    )
    return both[:, :128] + both[:, 128:]


def half_turn(block):
    return pltpu.roll(block, 64, 1)


def adjoint_step(loads, stores, tabs, h_same, h_cross):
    count = len(loads)
    low = lax.broadcasted_iota(jnp.int32, (256 * count, 128), 1) < 64
    sign = jnp.where(low, -1.0, 1.0)

    def rows(a, b):
        return jnp.concatenate([a, b], 0)

    reals, imags = [], []
    for load in loads:
        (x0r, x0i), (x1r, x1i), (x2r, x2i), (x3r, x3i) = [load(p) for p in range(4)]
        s0r, s0i, s1r, s1i = x0r + x2r, x0i + x2i, x1r + x3r, x1i + x3i
        d0r, d0i, d1r, d1i = x0r - x2r, x0i - x2i, x1r - x3r, x1i - x3i
        parts = (
            rows(s0r + s1r, s0i + s1i),
            rows(d0r + d1i, d0i - d1r),
            rows(s0r - s1r, s0i - s1i),
            rows(d0r - d1i, d0i + d1r),
        )
        for p in range(4):
            out = left_mul(tabs[0, p], parts[p])
            reals.append(out[:64])
            imags.append(out[64:])
    yr, yi = jnp.concatenate(reals, 0), jnp.concatenate(imags, 0)

    sr, si = yr[:, :128] + yr[:, 128:], yi[:, :128] + yi[:, 128:]
    dr, di = yr[:, :128] - yr[:, 128:], yi[:, :128] - yi[:, 128:]
    t = jnp.where(low, sr, si)
    u = half_turn(jnp.where(low, si, sr))
    v = half_turn(di)
    a, b = dr + v, dr - v
    parts = (t + u, jnp.where(low, a, b), t - u, jnp.where(low, b, a))
    back = []
    for k in range(4):
        z = right_mul(parts[k], tabs[1, k])
        w = half_turn(z)
        z = jnp.concatenate(
            [
                z[256 * n : 256 * n + 256] * h_same[k] + w[256 * n : 256 * n + 256] * h_cross[k]
                for n in range(count)
            ],
            0,
        )
        back.append(right_mul(z, tabs[2, k]))

    t = back[0] + back[2]
    u = half_turn(back[0] - back[2])
    er, ei = jnp.where(low, t, u), jnp.where(low, u, t)
    fr, fi = back[1] + back[3], half_turn(back[1] - back[3]) * sign
    xr = jnp.concatenate([er + fr, er - fr], 1)
    xi = jnp.concatenate([ei + fi, ei - fi], 1)
    for n in range(count):
        c = []
        for p in range(4):
            at = 256 * n + 64 * p
            out = left_mul(tabs[3, p], rows(xr[at : at + 64], xi[at : at + 64]))
            c.append((out[:64], out[64:]))
        (c0r, c0i), (c1r, c1i), (c2r, c2i), (c3r, c3i) = c
        e0r, e0i, e1r, e1i = c0r + c2r, c0i + c2i, c0r - c2r, c0i - c2i
        f0r, f0i, f1r, f1i = c1r + c3r, c1i + c3i, c3i - c1i, c1r - c3r
        stores[n](0, e0r + f0r, e0i + f0i)
        stores[n](1, e1r + f1r, e1i + f1i)
        stores[n](2, e0r - f0r, e0i - f0i)
        stores[n](3, e1r - f1r, e1i - f1i)


def quarter_at(p):
    return pl.ds(64 * p, 64)


def store_into(ref, angle):
    def store(p, real, imag):
        ref[angle, 0, quarter_at(p), :] = real
        ref[angle, 1, quarter_at(p), :] = imag

    return store


def half_range_cos_sin(turn):
    sq = turn * turn
    c = 1.0 / 479001600.0
    for n in (-1.0 / 3628800.0, 1.0 / 40320.0, -1.0 / 720.0, 1.0 / 24.0, -0.5, 1.0):
        c = c * sq + n
    s = -1.0 / 39916800.0
    for n in (1.0 / 362880.0, -1.0 / 5040.0, 1.0 / 120.0, -1.0 / 6.0, 1.0):
        s = s * sq + n
    return c, s * turn


def start_all(pairs, sems):
    copies = [pltpu.make_async_copy(a, b, sems.at[n]) for n, (a, b) in enumerate(pairs)]
    for copy in copies:
        copy.start()
    return copies


def first_kernel(dual, phase, tabs, mu, h_same, h_cross, lanes):
    row = lax.broadcasted_iota(jnp.int32, (256, 128), 0)
    lane = lax.broadcasted_iota(jnp.int32, (256, 128), 1)
    col = lane % 64 * 4
    sign = jnp.where(lane < 64, 1.0, -1.0)
    for n in range(2):
        lanes[pl.ds(256 * n, 256), :] = phase[:, pl.ds(128 * n, 128)]
    turn = jnp.concatenate(
        [
            jnp.concatenate([lanes[pl.ds(256 * n + q, 64, stride=4), :] for q in range(4)], 0)
            for n in range(2)
        ],
        1,
    )
    c, s = half_range_cos_sin(0.5 * turn)
    hr, hi = split(1.0 - 2.0 * s * s), split(2.0 * s * c)
    for k in range(4):
        pick = jnp.where(row == col + k, 1.0, 0.0).astype(jnp.bfloat16)
        same, cross = [
            sum(jnp.dot(term, pick, preferred_element_type=jnp.float32) for term in h)
            for h in (hr, hi)
        ]
        h_same[k] = same
        h_cross[k] = cross * sign

    def load_from(angle):
        return lambda p: (dual[angle, 0, quarter_at(p), :], dual[angle, 1, quarter_at(p), :])

    count = dual.shape[0]
    adjoint_step(
        [load_from(n) for n in range(count)],
        [store_into(mu, n) for n in range(count)],
        tabs,
        h_same,
        h_cross,
    )


def rest_kernel(
    mu_in, entry_in, h_same, h_cross, tabs, own, got, swapped, near, near_swapped,
    keep, send, mu, entry, tr, ti, sems,
):
    count = mu.shape[0]
    mu_copy, entry_copy = start_all(((mu_in, mu), (entry_in, entry)), sems)
    left = 3 - lax.axis_index("gz")
    core = lax.axis_index("angle") % 2

    def set_t(ref, at=slice(None)):
        c, s = half_range_cos_sin(PHASE_GAIN * ref[...])
        tr[at, :] = c
        ti[at, :] = s

    def set_t_for(step):
        one_above = (left != 2) & (left - step == 1)
        here = (step % 2) == core
        pl.when(~one_above & here)(lambda: set_t(got))
        pl.when(~one_above & ~here)(lambda: set_t(swapped))

        @pl.when(one_above)
        def _():
            set_t(near, pl.ds(pl.multiple_of(core * 128, 128), 128))
            set_t(near_swapped, pl.ds(pl.multiple_of(128 - core * 128, 128), 128))

    def load_from(angle):
        def load(p):
            at = quarter_at(p)
            r, i = mu[angle, 0, at, :], mu[angle, 1, at, :]
            return tr[at, :] * r + ti[at, :] * i, tr[at, :] * i - ti[at, :] * r

        return load

    set_t_for(0)
    mu_copy.wait()

    def one_slab(step, carry):
        pl.when(step > 0)(lambda: set_t_for(step))
        adjoint_step(
            [load_from(n) for n in range(count)],
            [store_into(mu, n) for n in range(count)],
            tabs,
            h_same,
            h_cross,
        )
        return carry

    lax.fori_loop(0, left, one_slab, 0)
    set_t(own)
    entry_copy.wait()

    def terms(at):
        gr = gi = 0.0
        for n in range(count):
            r, i = mu[n, 0, at, :], mu[n, 1, at, :]
            er, ei = entry[n, 0, at, :], entry[n, 1, at, :]
            gr += r * er + i * ei
            gi += i * er - r * ei
        return PHASE_GAIN * (tr[at, :] * gi - ti[at, :] * gr)

    for at in range(0, 128, 32):
        keep[pl.ds(at, 32), :] = terms(pl.ds(pl.multiple_of(core * 128 + at, 32), 32))
        send[pl.ds(at, 32), :] = terms(pl.ds(pl.multiple_of(128 - core * 128 + at, 32), 32))


def call(kernel, in_hbm, out_shape, scratch):
    return pl.pallas_call(
        kernel,
        out_shape=out_shape,
        in_specs=[pl.BlockSpec(memory_space=pl.ANY if far else pltpu.VMEM) for far in in_hbm],
        scratch_shapes=list(scratch),
        compiler_params=pltpu.CompilerParams(vmem_limit_bytes=VMEM_BYTES),
    )


def f32(*shape):
    return jax.ShapeDtypeStruct(shape, jnp.float32)


def angle_pairs(partner):
    pairs = []
    for n in range(64):
        z, y, x, c = partner(n // 32, n // 8 % 4, n // 2 % 4, n % 2)
        pairs.append((n, z * 32 + y * 8 + x * 2 + c))
    return pairs


def slab_pairs(moves):
    pairs = []
    for gz, core, gz_to, core_to, flip in moves:
        for n in range(core, 64, 2):
            pairs.append((gz * 64 + n, gz_to * 64 + ((n - core + core_to) ^ (32 * flip))))
    return pairs


def per_device(index, prop_phase, entry_field, exit_cotangent):
    count = exit_cotangent.shape[0]
    own = index[0]
    core = lax.axis_index("angle") % 2
    swap = angle_pairs(lambda z, y, x, c: (z, y, x, 1 - c))
    got = lax.ppermute(
        own,
        ("gz", "angle"),
        slab_pairs(((3, 0, 0, 0, 1), (2, 0, 0, 1, 0), (3, 1, 1, 0, 1), (2, 1, 1, 1, 0))),
    )
    mine = lax.dynamic_slice_in_dim(own, core * 128, 128, 0)
    near = lax.ppermute(
        mine,
        ("gz", "angle"),
        slab_pairs(((1, 0, 0, 0, 0), (1, 1, 0, 1, 0), (3, 0, 2, 0, 0), (3, 1, 2, 1, 0))),
    )
    field = (count, 2, 256, 256)
    h_shape = (4, 256, 128)
    tabs = call(
        tables_kernel, (), jax.ShapeDtypeStruct((4, 4, 256, 256), jnp.bfloat16), ()
    )()
    mu, h_same, h_cross = call(
        first_kernel,
        (False,) * 3,
        (f32(*field), f32(*h_shape), f32(*h_shape)),
        [pltpu.VMEM((512, 128), jnp.float32)],
    )(exit_cotangent, prop_phase, tabs)
    got, near, mu = lax.optimization_barrier((got, near, mu))
    swapped = lax.ppermute(got, "angle", swap)
    near_swapped = lax.ppermute(near, "angle", swap)
    fields = pltpu.VMEM(field, jnp.float32)
    plane = pltpu.VMEM((256, 256), jnp.float32)
    keep, send = call(
        rest_kernel,
        (True,) * 2 + (False,) * 8,
        (f32(128, 256), f32(128, 256)),
        [fields, fields, plane, plane, pltpu.SemaphoreType.DMA((2,))],
    )(mu, entry_field[0], h_same, h_cross, tabs, own, got, swapped, near, near_swapped)

    total = keep + lax.ppermute(send, "angle", swap)
    for ring in (
        (
            lambda z, y, x, c: (z, y, x ^ 2, c),
            lambda z, y, x, c: (z, y, 3 - x, c),
            lambda z, y, x, c: (z, y, x ^ 1, c),
        ),
        (
            lambda z, y, x, c: (z, y ^ 2, x, c),
            lambda z, y, x, c: (z, 3 - y, x, c),
            lambda z, y, x, c: (z, y ^ 1, x, c),
        ),
        (lambda z, y, x, c: (1 - z, y, x, c),),
    ):
        total = total + sum(lax.ppermute(total, "angle", angle_pairs(p)) for p in ring)
    angles = count * lax.axis_size("angle")
    new = jnp.maximum(mine - UPDATE_RATE * (total / angles), 0.0)
    other = lax.ppermute(new, "angle", swap)
    return jnp.where(
        core == 0, jnp.concatenate([new, other], 0), jnp.concatenate([other, new], 0)
    )[None]


def solution(mesh):
    return jax.shard_map(
        per_device,
        mesh=mesh,
        in_specs=(
            P("gz", None, None),
            P(),
            P("gz", "angle", None, None, None),
            P("angle", None, None, None),
        ),
        out_specs=P("gz", None, None),
        check_vma=False,
    )
```

```python
import math

import jax
import jax.numpy as jnp
from jax import lax
from jax.experimental import pallas as pl
from jax.experimental.pallas import tpu as pltpu
from jax.sharding import PartitionSpec as P

PHASE_GAIN = 2.0
UPDATE_RATE = 4.0
VMEM_BYTES = 28 * 2**20


def tables_kernel(tabs):
    row = lax.broadcasted_iota(jnp.int32, (128, 128), 0)
    lane = lax.broadcasted_iota(jnp.int32, (128, 128), 1)
    zero = jnp.zeros((128, 128), jnp.bfloat16)
    for n in range(4):
        for which in range(2):
            m, j = (row % 64, lane % 64) if which == 0 else (lane % 64, row % 64)
            turn = (n * j + 4 * m * j + 128) % 256 - 128
            c, s = half_range_cos_sin(turn.astype(jnp.float32) * (math.pi / 256.0))
            cos, sin = (1.0 - 2.0 * s * s) / 16.0, 2.0 * s * c / 16.0
            upper, right = row < 64, lane >= 64
            cross = jnp.where(upper, sin, -sin)
            real = jnp.where(upper != right, cos, cross if which == 0 else -cross)
            for to in ((0, 2), (3, 1))[which]:
                flipped = real
                if n in (1, 2) and to in (1, 2):
                    flipped = jnp.where((row if to == 1 else lane) < 64, real, -real)
                high, low = split(flipped)
                on_left = to in (0, 3)
                tabs[to, n, :128, :128] = high
                tabs[to, n, :128, 128:] = high if on_left else low
                tabs[to, n, 128:, :128] = low if on_left else high
                tabs[to, n, 128:, 128:] = zero


def split(block):
    high = block.astype(jnp.bfloat16)
    return high, (block - high.astype(jnp.float32)).astype(jnp.bfloat16)


def left_mul(matrix, block):
    both = jnp.dot(
        matrix, jnp.concatenate(split(block), 0), preferred_element_type=jnp.float32
    )
    return both[:128] + both[128:]


def right_mul(block, matrix):
    both = jnp.dot(
        jnp.concatenate(split(block), 1), matrix, preferred_element_type=jnp.float32
    )
    return both[:, :128] + both[:, 128:]


def half_turn(block):
    return pltpu.roll(block, 64, 1)


def adjoint_step(loads, stores, tabs, h_same, h_cross):
    count = len(loads)
    low = lax.broadcasted_iota(jnp.int32, (256 * count, 128), 1) < 64
    sign = jnp.where(low, -1.0, 1.0)

    def rows(a, b):
        return jnp.concatenate([a, b], 0)

    reals, imags = [], []
    for load in loads:
        (x0r, x0i), (x1r, x1i), (x2r, x2i), (x3r, x3i) = [load(p) for p in range(4)]
        s0r, s0i, s1r, s1i = x0r + x2r, x0i + x2i, x1r + x3r, x1i + x3i
        d0r, d0i, d1r, d1i = x0r - x2r, x0i - x2i, x1r - x3r, x1i - x3i
        parts = (
            rows(s0r + s1r, s0i + s1i),
            rows(d0r + d1i, d0i - d1r),
            rows(s0r - s1r, s0i - s1i),
            rows(d0r - d1i, d0i + d1r),
        )
        for p in range(4):
            out = left_mul(tabs[0, p], parts[p])
            reals.append(out[:64])
            imags.append(out[64:])
    yr, yi = jnp.concatenate(reals, 0), jnp.concatenate(imags, 0)

    sr, si = yr[:, :128] + yr[:, 128:], yi[:, :128] + yi[:, 128:]
    dr, di = yr[:, :128] - yr[:, 128:], yi[:, :128] - yi[:, 128:]
    t = jnp.where(low, sr, si)
    u = half_turn(jnp.where(low, si, sr))
    v = half_turn(di)
    a, b = dr + v, dr - v
    parts = (t + u, jnp.where(low, a, b), t - u, jnp.where(low, b, a))
    back = []
    for k in range(4):
        z = right_mul(parts[k], tabs[1, k])
        w = half_turn(z)
        z = jnp.concatenate(
            [
                z[256 * n : 256 * n + 256] * h_same[k] + w[256 * n : 256 * n + 256] * h_cross[k]
                for n in range(count)
            ],
            0,
        )
        back.append(right_mul(z, tabs[2, k]))

    t = back[0] + back[2]
    u = half_turn(back[0] - back[2])
    er, ei = jnp.where(low, t, u), jnp.where(low, u, t)
    fr, fi = back[1] + back[3], half_turn(back[1] - back[3]) * sign
    xr = jnp.concatenate([er + fr, er - fr], 1)
    xi = jnp.concatenate([ei + fi, ei - fi], 1)
    for n in range(count):
        c = []
        for p in range(4):
            at = 256 * n + 64 * p
            out = left_mul(tabs[3, p], rows(xr[at : at + 64], xi[at : at + 64]))
            c.append((out[:64], out[64:]))
        (c0r, c0i), (c1r, c1i), (c2r, c2i), (c3r, c3i) = c
        e0r, e0i, e1r, e1i = c0r + c2r, c0i + c2i, c0r - c2r, c0i - c2i
        f0r, f0i, f1r, f1i = c1r + c3r, c1i + c3i, c3i - c1i, c1r - c3r
        stores[n](0, e0r + f0r, e0i + f0i)
        stores[n](1, e1r + f1r, e1i + f1i)
        stores[n](2, e0r - f0r, e0i - f0i)
        stores[n](3, e1r - f1r, e1i - f1i)


def quarter_at(p):
    return pl.ds(64 * p, 64)


def store_into(ref, angle):
    def store(p, real, imag):
        ref[angle, 0, quarter_at(p), :] = real
        ref[angle, 1, quarter_at(p), :] = imag

    return store


def half_range_cos_sin(turn):
    sq = turn * turn
    c = 1.0 / 479001600.0
    for n in (-1.0 / 3628800.0, 1.0 / 40320.0, -1.0 / 720.0, 1.0 / 24.0, -0.5, 1.0):
        c = c * sq + n
    s = -1.0 / 39916800.0
    for n in (1.0 / 362880.0, -1.0 / 5040.0, 1.0 / 120.0, -1.0 / 6.0, 1.0):
        s = s * sq + n
    return c, s * turn


def set_t(plane, tr, ti, at=slice(None)):
    c, s = half_range_cos_sin(PHASE_GAIN * plane[...])
    tr[at, :] = c
    ti[at, :] = s


def first_kernel(dual, phase, tabs, own, mu, h_same, h_cross, own_tr, own_ti, lanes):
    set_t(own, own_tr, own_ti)
    row = lax.broadcasted_iota(jnp.int32, (256, 128), 0)
    lane = lax.broadcasted_iota(jnp.int32, (256, 128), 1)
    col = lane % 64 * 4
    sign = jnp.where(lane < 64, 1.0, -1.0)
    for n in range(2):
        lanes[pl.ds(256 * n, 256), :] = phase[:, pl.ds(128 * n, 128)]
    turn = jnp.concatenate(
        [
            jnp.concatenate([lanes[pl.ds(256 * n + q, 64, stride=4), :] for q in range(4)], 0)
            for n in range(2)
        ],
        1,
    )
    c, s = half_range_cos_sin(0.5 * turn)
    hr, hi = split(1.0 - 2.0 * s * s), split(2.0 * s * c)
    for k in range(4):
        pick = jnp.where(row == col + k, 1.0, 0.0).astype(jnp.bfloat16)
        same, cross = [
            sum(jnp.dot(term, pick, preferred_element_type=jnp.float32) for term in h)
            for h in (hr, hi)
        ]
        h_same[k] = same
        h_cross[k] = cross * sign

    def load_from(angle):
        return lambda p: (dual[angle, 0, quarter_at(p), :], dual[angle, 1, quarter_at(p), :])

    count = dual.shape[0]
    adjoint_step(
        [load_from(n) for n in range(count)],
        [store_into(mu, n) for n in range(count)],
        tabs,
        h_same,
        h_cross,
    )


def rest_kernel(
    mu_in, entry, h_same, h_cross, tabs, own_tr, own_ti, got, swapped, near, near_swapped,
    keep, send, mu, tr, ti,
):
    count = mu.shape[0]
    left = 3 - lax.axis_index("gz")
    core = lax.axis_index("angle") % 2

    def set_t_for(step):
        one_above = (left != 2) & (left - step == 1)
        here = (step % 2) == core
        pl.when(~one_above & here)(lambda: set_t(got, tr, ti))
        pl.when(~one_above & ~here)(lambda: set_t(swapped, tr, ti))

        @pl.when(one_above)
        def _():
            set_t(near, tr, ti, pl.ds(pl.multiple_of(core * 128, 128), 128))
            set_t(near_swapped, tr, ti, pl.ds(pl.multiple_of(128 - core * 128, 128), 128))

    def load_from(ref, angle):
        def load(p):
            at = quarter_at(p)
            r, i = ref[angle, 0, at, :], ref[angle, 1, at, :]
            return tr[at, :] * r + ti[at, :] * i, tr[at, :] * i - ti[at, :] * r

        return load

    def one_slab(step, ref):
        set_t_for(step)
        adjoint_step(
            [load_from(ref, n) for n in range(count)],
            [store_into(mu, n) for n in range(count)],
            tabs,
            h_same,
            h_cross,
        )

    @pl.when(left > 0)
    def _():
        one_slab(0, mu_in)

    @pl.when(left == 0)
    def _():
        mu[...] = mu_in[...]

    lax.fori_loop(1, left, lambda step, _: one_slab(step, mu), None)

    def terms(at):
        gr = gi = 0.0
        for n in range(count):
            r, i = mu[n, 0, at, :], mu[n, 1, at, :]
            er, ei = entry[n, 0, at, :], entry[n, 1, at, :]
            gr += r * er + i * ei
            gi += i * er - r * ei
        return PHASE_GAIN * (own_tr[at, :] * gi - own_ti[at, :] * gr)

    for at in range(0, 128, 32):
        keep[pl.ds(at, 32), :] = terms(pl.ds(pl.multiple_of(core * 128 + at, 32), 32))
        send[pl.ds(at, 32), :] = terms(pl.ds(pl.multiple_of(128 - core * 128 + at, 32), 32))


def call(kernel, in_hbm, out_shape, scratch):
    return pl.pallas_call(
        kernel,
        out_shape=out_shape,
        in_specs=[pl.BlockSpec(memory_space=pl.ANY if far else pltpu.VMEM) for far in in_hbm],
        scratch_shapes=list(scratch),
        compiler_params=pltpu.CompilerParams(vmem_limit_bytes=VMEM_BYTES),
    )


def f32(*shape):
    return jax.ShapeDtypeStruct(shape, jnp.float32)


def angle_pairs(partner):
    pairs = []
    for n in range(64):
        z, y, x, c = partner(n // 32, n // 8 % 4, n // 2 % 4, n % 2)
        pairs.append((n, z * 32 + y * 8 + x * 2 + c))
    return pairs


def slab_pairs(moves):
    pairs = []
    for gz, core, gz_to, core_to, flip in moves:
        for n in range(core, 64, 2):
            pairs.append((gz * 64 + n, gz_to * 64 + ((n - core + core_to) ^ (32 * flip))))
    return pairs


def per_device(index, prop_phase, entry_field, exit_cotangent):
    count = exit_cotangent.shape[0]
    own = index[0]
    core = lax.axis_index("angle") % 2
    swap = angle_pairs(lambda z, y, x, c: (z, y, x, 1 - c))
    got = lax.ppermute(
        own,
        ("gz", "angle"),
        slab_pairs(((3, 0, 0, 0, 1), (2, 0, 0, 1, 0), (3, 1, 1, 0, 1), (2, 1, 1, 1, 0))),
    )
    mine = lax.dynamic_slice_in_dim(own, core * 128, 128, 0)
    near = lax.ppermute(
        mine,
        ("gz", "angle"),
        slab_pairs(((1, 0, 0, 0, 0), (1, 1, 0, 1, 0), (3, 0, 2, 0, 0), (3, 1, 2, 1, 0))),
    )
    field = (count, 2, 256, 256)
    h_shape = (4, 256, 128)
    tabs = call(
        tables_kernel, (), jax.ShapeDtypeStruct((4, 4, 256, 256), jnp.bfloat16), ()
    )()
    mu, h_same, h_cross, own_tr, own_ti = call(
        first_kernel,
        (False,) * 4,
        (f32(*field), f32(*h_shape), f32(*h_shape), f32(256, 256), f32(256, 256)),
        [pltpu.VMEM((512, 128), jnp.float32)],
    )(exit_cotangent, prop_phase, tabs, own)
    got, near, mu = lax.optimization_barrier((got, near, mu))
    swapped = lax.ppermute(got, "angle", swap)
    near_swapped = lax.ppermute(near, "angle", swap)
    fields = pltpu.VMEM(field, jnp.float32)
    plane = pltpu.VMEM((256, 256), jnp.float32)
    keep, send = call(
        rest_kernel,
        (False,) * 11,
        (f32(128, 256), f32(128, 256)),
        [fields, plane, plane],
    )(
        mu, entry_field[0], h_same, h_cross, tabs, own_tr, own_ti,
        got, swapped, near, near_swapped,
    )

    total = keep + lax.ppermute(send, "angle", swap)
    for ring in (
        (
            lambda z, y, x, c: (z, y, x ^ 2, c),
            lambda z, y, x, c: (z, y, x ^ 1, c),
            lambda z, y, x, c: (z, y, 3 - x, c),
        ),
        (
            lambda z, y, x, c: (z, y ^ 2, x, c),
            lambda z, y, x, c: (z, y ^ 1, x, c),
            lambda z, y, x, c: (z, 3 - y, x, c),
        ),
        (lambda z, y, x, c: (1 - z, y, x, c),),
    ):
        total = total + sum(lax.ppermute(total, "angle", angle_pairs(p)) for p in ring)
    angles = count * lax.axis_size("angle")
    new = jnp.maximum(mine - UPDATE_RATE * (total / angles), 0.0)
    other = lax.ppermute(new, "angle", swap)
    return jnp.where(
        core == 0, jnp.concatenate([new, other], 0), jnp.concatenate([other, new], 0)
    )[None]


def solution(mesh):
    return jax.shard_map(
        per_device,
        mesh=mesh,
        in_specs=(
            P("gz", None, None),
            P(),
            P("gz", "angle", None, None, None),
            P("angle", None, None, None),
        ),
        out_specs=P("gz", None, None),
        check_vma=False,
    )
```

```python
import math

import jax
import jax.numpy as jnp
from jax import lax
from jax.experimental import pallas as pl
from jax.experimental.pallas import tpu as pltpu
from jax.sharding import PartitionSpec as P

PHASE_GAIN = 2.0
UPDATE_RATE = 4.0
VMEM_BYTES = 28 * 2**20


def tables_kernel(tabs):
    row = lax.broadcasted_iota(jnp.int32, (128, 128), 0)
    lane = lax.broadcasted_iota(jnp.int32, (128, 128), 1)
    zero = jnp.zeros((128, 128), jnp.bfloat16)
    for n in range(4):
        for which in range(2):
            m, j = (row % 64, lane % 64) if which == 0 else (lane % 64, row % 64)
            turn = (n * j + 4 * m * j + 128) % 256 - 128
            c, s = half_range_cos_sin(turn.astype(jnp.float32) * (math.pi / 256.0))
            cos, sin = (1.0 - 2.0 * s * s) / 16.0, 2.0 * s * c / 16.0
            upper, right = row < 64, lane >= 64
            cross = jnp.where(upper, sin, -sin)
            real = jnp.where(upper != right, cos, cross if which == 0 else -cross)
            for to in ((0, 2), (3, 1))[which]:
                flipped = real
                if n in (1, 2) and to in (1, 2):
                    flipped = jnp.where((row if to == 1 else lane) < 64, real, -real)
                high, low = split(flipped)
                on_left = to in (0, 3)
                tabs[to, n, :128, :128] = high
                tabs[to, n, :128, 128:] = high if on_left else low
                tabs[to, n, 128:, :128] = low if on_left else high
                tabs[to, n, 128:, 128:] = zero


def split(block):
    high = block.astype(jnp.bfloat16)
    return high, (block - high.astype(jnp.float32)).astype(jnp.bfloat16)


def left_mul(matrix, block):
    both = jnp.dot(
        matrix, jnp.concatenate(split(block), 0), preferred_element_type=jnp.float32
    )
    return both[:128] + both[128:]


def right_mul(block, matrix):
    both = jnp.dot(
        jnp.concatenate(split(block), 1), matrix, preferred_element_type=jnp.float32
    )
    return both[:, :128] + both[:, 128:]


def half_turn(block):
    return pltpu.roll(block, 64, 1)


def adjoint_step(loads, stores, tabs, h_same, h_cross):
    count = len(loads)
    low = lax.broadcasted_iota(jnp.int32, (256 * count, 128), 1) < 64
    sign = jnp.where(low, -1.0, 1.0)

    def rows(a, b):
        return jnp.concatenate([a, b], 0)

    reals, imags = [], []
    for load in loads:
        (x0r, x0i), (x1r, x1i), (x2r, x2i), (x3r, x3i) = [load(p) for p in range(4)]
        s0r, s0i, s1r, s1i = x0r + x2r, x0i + x2i, x1r + x3r, x1i + x3i
        d0r, d0i, d1r, d1i = x0r - x2r, x0i - x2i, x1r - x3r, x1i - x3i
        parts = (
            rows(s0r + s1r, s0i + s1i),
            rows(d0r + d1i, d0i - d1r),
            rows(s0r - s1r, s0i - s1i),
            rows(d0r - d1i, d0i + d1r),
        )
        for p in range(4):
            out = left_mul(tabs[0, p], parts[p])
            reals.append(out[:64])
            imags.append(out[64:])
    yr, yi = jnp.concatenate(reals, 0), jnp.concatenate(imags, 0)

    sr, si = yr[:, :128] + yr[:, 128:], yi[:, :128] + yi[:, 128:]
    dr, di = yr[:, :128] - yr[:, 128:], yi[:, :128] - yi[:, 128:]
    t = jnp.where(low, sr, si)
    u = half_turn(jnp.where(low, si, sr))
    v = half_turn(di)
    a, b = dr + v, dr - v
    parts = (t + u, jnp.where(low, a, b), t - u, jnp.where(low, b, a))
    back = []
    for k in range(4):
        z = right_mul(parts[k], tabs[1, k])
        w = half_turn(z)
        z = jnp.concatenate(
            [
                z[256 * n : 256 * n + 256] * h_same[k] + w[256 * n : 256 * n + 256] * h_cross[k]
                for n in range(count)
            ],
            0,
        )
        back.append(right_mul(z, tabs[2, k]))

    t = back[0] + back[2]
    u = half_turn(back[0] - back[2])
    er, ei = jnp.where(low, t, u), jnp.where(low, u, t)
    fr, fi = back[1] + back[3], half_turn(back[1] - back[3]) * sign
    xr = jnp.concatenate([er + fr, er - fr], 1)
    xi = jnp.concatenate([ei + fi, ei - fi], 1)
    for n in range(count):
        c = []
        for p in range(4):
            at = 256 * n + 64 * p
            out = left_mul(tabs[3, p], rows(xr[at : at + 64], xi[at : at + 64]))
            c.append((out[:64], out[64:]))
        (c0r, c0i), (c1r, c1i), (c2r, c2i), (c3r, c3i) = c
        e0r, e0i, e1r, e1i = c0r + c2r, c0i + c2i, c0r - c2r, c0i - c2i
        f0r, f0i, f1r, f1i = c1r + c3r, c1i + c3i, c3i - c1i, c1r - c3r
        stores[n](0, e0r + f0r, e0i + f0i)
        stores[n](1, e1r + f1r, e1i + f1i)
        stores[n](2, e0r - f0r, e0i - f0i)
        stores[n](3, e1r - f1r, e1i - f1i)


def quarter_at(p):
    return pl.ds(64 * p, 64)


def store_into(ref, angle):
    def store(p, real, imag):
        ref[angle, 0, quarter_at(p), :] = real
        ref[angle, 1, quarter_at(p), :] = imag

    return store


def half_range_cos_sin(turn):
    sq = turn * turn
    c = 1.0 / 479001600.0
    for n in (-1.0 / 3628800.0, 1.0 / 40320.0, -1.0 / 720.0, 1.0 / 24.0, -0.5, 1.0):
        c = c * sq + n
    s = -1.0 / 39916800.0
    for n in (1.0 / 362880.0, -1.0 / 5040.0, 1.0 / 120.0, -1.0 / 6.0, 1.0):
        s = s * sq + n
    return c, s * turn


def set_t(plane, tr, ti, at=slice(None)):
    c, s = half_range_cos_sin(PHASE_GAIN * plane[...])
    tr[at, :] = c
    ti[at, :] = s


def first_kernel(dual, phase, tabs, own, mu, h_same, h_cross, own_tr, own_ti, lanes):
    set_t(own, own_tr, own_ti)
    row = lax.broadcasted_iota(jnp.int32, (256, 128), 0)
    lane = lax.broadcasted_iota(jnp.int32, (256, 128), 1)
    col = lane % 64 * 4
    sign = jnp.where(lane < 64, 1.0, -1.0)
    for n in range(2):
        lanes[pl.ds(256 * n, 256), :] = phase[:, pl.ds(128 * n, 128)]
    turn = jnp.concatenate(
        [
            jnp.concatenate([lanes[pl.ds(256 * n + q, 64, stride=4), :] for q in range(4)], 0)
            for n in range(2)
        ],
        1,
    )
    c, s = half_range_cos_sin(0.5 * turn)
    hr, hi = split(1.0 - 2.0 * s * s), split(2.0 * s * c)
    for k in range(4):
        pick = jnp.where(row == col + k, 1.0, 0.0).astype(jnp.bfloat16)
        same, cross = [
            sum(jnp.dot(term, pick, preferred_element_type=jnp.float32) for term in h)
            for h in (hr, hi)
        ]
        h_same[k] = same
        h_cross[k] = cross * sign

    def load_from(angle):
        return lambda p: (dual[angle, 0, quarter_at(p), :], dual[angle, 1, quarter_at(p), :])

    count = dual.shape[0]
    adjoint_step(
        [load_from(n) for n in range(count)],
        [store_into(mu, n) for n in range(count)],
        tabs,
        h_same,
        h_cross,
    )


def rest_kernel(
    mu_in, entry, h_same, h_cross, tabs, own_tr, own_ti, got, swapped, near, near_swapped,
    keep, send, mu, tr, ti,
):
    count = mu.shape[0]
    left = 3 - lax.axis_index("gz")
    core = lax.axis_index("angle") % 2

    def set_t_for(step):
        one_above = (left != 2) & (left - step == 1)
        here = (step % 2) == core
        pl.when(~one_above & here)(lambda: set_t(got, tr, ti))
        pl.when(~one_above & ~here)(lambda: set_t(swapped, tr, ti))

        @pl.when(one_above)
        def _():
            set_t(near, tr, ti, pl.ds(pl.multiple_of(core * 128, 128), 128))
            set_t(near_swapped, tr, ti, pl.ds(pl.multiple_of(128 - core * 128, 128), 128))

    def load_from(ref, angle):
        def load(p):
            at = quarter_at(p)
            r, i = ref[angle, 0, at, :], ref[angle, 1, at, :]
            return tr[at, :] * r + ti[at, :] * i, tr[at, :] * i - ti[at, :] * r

        return load

    def one_slab(step, ref):
        set_t_for(step)
        adjoint_step(
            [load_from(ref, n) for n in range(count)],
            [store_into(mu, n) for n in range(count)],
            tabs,
            h_same,
            h_cross,
        )

    @pl.when(left > 0)
    def _():
        one_slab(0, mu_in)

    @pl.when(left == 0)
    def _():
        mu[...] = mu_in[...]

    lax.fori_loop(1, left, lambda step, _: one_slab(step, mu), None)

    def terms(at):
        gr = gi = 0.0
        for n in range(count):
            r, i = mu[n, 0, at, :], mu[n, 1, at, :]
            er, ei = entry[n, 0, at, :], entry[n, 1, at, :]
            gr += r * er + i * ei
            gi += i * er - r * ei
        return PHASE_GAIN * (own_tr[at, :] * gi - own_ti[at, :] * gr)

    for at in range(0, 128, 32):
        keep[pl.ds(at, 32), :] = terms(pl.ds(pl.multiple_of(core * 128 + at, 32), 32))
        send[pl.ds(at, 32), :] = terms(pl.ds(pl.multiple_of(128 - core * 128 + at, 32), 32))


def call(kernel, in_hbm, out_shape, scratch):
    return pl.pallas_call(
        kernel,
        out_shape=out_shape,
        in_specs=[pl.BlockSpec(memory_space=pl.ANY if far else pltpu.VMEM) for far in in_hbm],
        scratch_shapes=list(scratch),
        compiler_params=pltpu.CompilerParams(vmem_limit_bytes=VMEM_BYTES),
    )


def f32(*shape):
    return jax.ShapeDtypeStruct(shape, jnp.float32)


def angle_pairs(partner):
    pairs = []
    for n in range(64):
        z, y, x, c = partner(n // 32, n // 8 % 4, n // 2 % 4, n % 2)
        pairs.append((n, z * 32 + y * 8 + x * 2 + c))
    return pairs


def slab_pairs(moves):
    pairs = []
    for gz, core, gz_to, core_to, flip in moves:
        for n in range(core, 64, 2):
            pairs.append((gz * 64 + n, gz_to * 64 + ((n - core + core_to) ^ (32 * flip))))
    return pairs


def per_device(index, prop_phase, entry_field, exit_cotangent):
    count = exit_cotangent.shape[0]
    own = index[0]
    core = lax.axis_index("angle") % 2
    swap = angle_pairs(lambda z, y, x, c: (z, y, x, 1 - c))
    got = lax.ppermute(
        own,
        ("gz", "angle"),
        slab_pairs(((3, 0, 0, 0, 0), (2, 0, 0, 1, 1), (3, 1, 1, 0, 1), (2, 1, 1, 1, 0))),
    )
    mine = lax.dynamic_slice_in_dim(own, core * 128, 128, 0)
    near = lax.ppermute(
        mine,
        ("gz", "angle"),
        slab_pairs(((1, 0, 0, 0, 0), (1, 1, 0, 1, 0), (3, 0, 2, 0, 0), (3, 1, 2, 1, 0))),
    )
    field = (count, 2, 256, 256)
    h_shape = (4, 256, 128)
    tabs = call(
        tables_kernel, (), jax.ShapeDtypeStruct((4, 4, 256, 256), jnp.bfloat16), ()
    )()
    mu, h_same, h_cross, own_tr, own_ti = call(
        first_kernel,
        (False,) * 4,
        (f32(*field), f32(*h_shape), f32(*h_shape), f32(256, 256), f32(256, 256)),
        [pltpu.VMEM((512, 128), jnp.float32)],
    )(exit_cotangent, prop_phase, tabs, own)
    got, near, mu = lax.optimization_barrier((got, near, mu))
    swapped = lax.ppermute(got, "angle", swap)
    near_swapped = lax.ppermute(near, "angle", swap)
    fields = pltpu.VMEM(field, jnp.float32)
    plane = pltpu.VMEM((256, 256), jnp.float32)
    keep, send = call(
        rest_kernel,
        (False,) * 11,
        (f32(128, 256), f32(128, 256)),
        [fields, plane, plane],
    )(
        mu, entry_field[0], h_same, h_cross, tabs, own_tr, own_ti,
        got, swapped, near, near_swapped,
    )

    total = keep + lax.ppermute(send, "angle", swap)
    for ring in (
        (
            lambda z, y, x, c: (z, y, x ^ 2, c),
            lambda z, y, x, c: (z, y, x ^ 1, c),
            lambda z, y, x, c: (z, y, 3 - x, c),
        ),
        (
            lambda z, y, x, c: (z, y ^ 2, x, c),
            lambda z, y, x, c: (z, y ^ 1, x, c),
            lambda z, y, x, c: (z, 3 - y, x, c),
        ),
        (lambda z, y, x, c: (1 - z, y, x, c),),
    ):
        total = total + sum(lax.ppermute(total, "angle", angle_pairs(p)) for p in ring)
    angles = count * lax.axis_size("angle")
    new = jnp.maximum(mine - UPDATE_RATE * (total / angles), 0.0)
    other = lax.ppermute(new, "angle", swap)
    return jnp.where(
        core == 0, jnp.concatenate([new, other], 0), jnp.concatenate([other, new], 0)
    )[None]


def solution(mesh):
    return jax.shard_map(
        per_device,
        mesh=mesh,
        in_specs=(
            P("gz", None, None),
            P(),
            P("gz", "angle", None, None, None),
            P("angle", None, None, None),
        ),
        out_specs=P("gz", None, None),
        check_vma=False,
    )
```
